32 devices in a mesh: seq: 8 (over z, y), head: 4 (over x, core).
Axes of the slice: x: 2, y: 2, z: 4, core: 2. Of those that a mesh axis runs over, the one named last changes fastest.
Arguments:
- queries: bfloat16 [8192, 3072], P('seq', 'head'), may hold values from -10 to 10
- keys: bfloat16 [8192, 3072], P('seq', 'head'), may hold values from -4 to 4
- values: bfloat16 [8192, 3072], P('seq', 'head'), may hold values from -4 to 4
- w_out: bfloat16 [3072, 3072], P('head', 'seq'), may hold values from -0.21875 to 0.21875
- head_kind: int32 [24], replicated, may hold values from 0 to 1, as said below
- band_offsets: int32 [2, 7], replicated, may hold values from -4 to 4, as said below
Outputs:
- mixed: bfloat16 [8192, 3072], P(('seq', 'head'))
The draws below stay inside these ranges and needn't reach their ends.
Inputs may be any that keep to these rules, and one draw needn't show every extreme that they name: `head_kind`: each group of 6 consecutive heads holds at most 5 temporal heads, and some group holds exactly that many. `band_offsets`: each row holds 7 distinct offsets and always contains 0, 4 and minus 4.
All inputs are finite; a program needn't handle non-finite values.
Results may differ from the reference program's by a relative error of at most 0.013.
Values may be sent and summed in bfloat16 or wider, within the bound.
No kernel may reach another device: no remote copies, remote signals or barrier semaphores. Data moves between devices by JAX's collectives and lax.ppermute only.
A program may use at most 128 MiB of HBM per device.

```python
import math
import jax
import jax.numpy as jnp
from jax import lax

D = 3072
HEADS = 24
DH = 128
FRAMES = 16
BLK = 256
KOFF = 7
TOKENS = 8192
POSITIONS = 512
RUN = 512
QUOTA = 64
HEAD_DEV = 6
SPAN = 4
ATT = 3072
N_SEQ = 8
N_HEAD = 4


def draw_queries(key, part):
    noise = jax.random.normal(jax.random.fold_in(key, 11), (TOKENS, ATT)) * 2.5
    result = jnp.clip(noise, -10.0, 10.0)
    return result.astype(jnp.bfloat16)


def draw_keys(key, part):
    noise = jax.random.normal(jax.random.fold_in(key, 13), (TOKENS, ATT))
    result = jnp.clip(noise, -4.0, 4.0)
    return result.astype(jnp.bfloat16)


def draw_head_kind(key, part):
    groups = HEADS // HEAD_DEV
    counts = jax.random.randint(jax.random.fold_in(key, 21), (groups,), 0, HEAD_DEV)
    forced = jax.random.randint(jax.random.fold_in(key, 22), (), 0, groups)
    counts = jnp.where(jnp.arange(groups) == forced, HEAD_DEV - 1, counts)
    group_keys = jax.random.split(jax.random.fold_in(key, 23), groups)
    ranking = jax.vmap(lambda group_key: jax.random.permutation(group_key, HEAD_DEV))(group_keys)
    return (ranking < counts[:, None]).astype(jnp.int32).reshape(HEADS)


def draw_band_offsets(key, part):
    inner_steps = jnp.arange(1, SPAN, dtype=jnp.int32)
    candidates = jnp.concatenate([-inner_steps, inner_steps])
    fixed_part = jnp.array([0, -SPAN, SPAN], dtype=jnp.int32)
    offset_rows = []
    for head_type in range(2):
        picked = jax.random.permutation(jax.random.fold_in(key, 31 + head_type), candidates)[:KOFF - 3]
        offset_rows.append(jnp.concatenate([fixed_part, picked.astype(jnp.int32)]))
    return jnp.stack(offset_rows)


def block_levels(stream_key, extent, cuts, low, high):
    level, own = 1.0, jax.random.fold_in(stream_key, 6)
    for position, parts in cuts:
        draws = jnp.exp(jax.random.uniform(jax.random.fold_in(own, position), (parts,), jnp.float32, low / len(cuts), high / len(cuts)))
        level = level * jnp.repeat(draws, extent[position] // parts).reshape([-1 if axis == position else 1 for axis in range(len(extent))])
    return level


def scatter_about(stream_key, shape, deviation, most, pieces=(), held_as=jnp.bfloat16):
    level = block_levels(stream_key, shape, pieces, -0.22, 0.18) if pieces else 1.0
    values = jax.random.normal(stream_key, shape, jnp.float32) * deviation * level
    return jnp.minimum(jnp.maximum(values, -most), most).astype(held_as)


def setup_inputs(seed: int = 0) -> dict:
    arg_keys = jax.random.split(jax.random.key(seed), 7)
    return {
        "queries": draw_queries(jax.random.fold_in(arg_keys[6], 71), 0),
        "keys": draw_keys(jax.random.fold_in(arg_keys[6], 71), 0),
        "values": scatter_about(arg_keys[2], (TOKENS, ATT), 1.0, 4.0, ((0, 8), (1, 4))),
        "w_out": scatter_about(arg_keys[3], (ATT, D), (ATT // 4) ** -0.5, 0.21875, ((0, 4), (1, 8))),
        "head_kind": draw_head_kind(jax.random.fold_in(arg_keys[6], 71), 0),
        "band_offsets": draw_band_offsets(jax.random.fold_in(arg_keys[6], 71), 0),
    }


def to_temporal(field_rows):
    channels = field_rows.shape[1]
    grid_view = field_rows.reshape(FRAMES, POSITIONS // RUN, N_SEQ, QUOTA, channels)
    return grid_view.transpose(2, 1, 3, 0, 4).reshape(TOKENS, channels)

def from_temporal(field_rows):
    channels = field_rows.shape[1]
    grid_view = field_rows.reshape(N_SEQ, POSITIONS // RUN, QUOTA, FRAMES, channels)
    return grid_view.transpose(3, 1, 0, 2, 4).reshape(TOKENS, channels)

def band_attend(query_rows, key_rows, value_rows, offsets):
    block_count = TOKENS // BLK
    query_blocks = query_rows.reshape(block_count, BLK, DH)
    k_blocks = key_rows.reshape(block_count, BLK, DH)
    v_blocks = value_rows.reshape(block_count, BLK, DH)
    target = jnp.arange(block_count, dtype=jnp.int32)[:, None] + offsets[None, :]
    in_range = (target >= 0) & (target < block_count)
    key_index = jnp.clip(target, 0, block_count - 1).astype(jnp.int32)
    nearby_keys = jnp.take(k_blocks, key_index, axis=0).reshape(block_count, KOFF * BLK, DH)
    nearby_values = jnp.take(v_blocks, key_index, axis=0).reshape(block_count, KOFF * BLK, DH)
    score_scale = 1.0 / math.sqrt(DH)
    attention_scores = jnp.einsum('vuf,vzf->vuz', query_blocks.astype(jnp.float32), nearby_keys.astype(jnp.float32)) * score_scale
    allowed = jnp.broadcast_to(in_range[:, :, None], (block_count, KOFF, BLK)).reshape(block_count, 1, KOFF * BLK)
    attention_scores = jnp.where(allowed, attention_scores, -1e+30)
    row_max = lax.optimization_barrier(jnp.max(attention_scores, axis=2, keepdims=True))
    weights = jnp.exp(attention_scores - row_max)
    attention_probabilities = (weights / lax.optimization_barrier(jnp.sum(weights, axis=2, keepdims=True))).astype(jnp.bfloat16)
    attended_output = jnp.einsum('oyx,oxi->oyi', attention_probabilities.astype(jnp.float32), nearby_values.astype(jnp.float32))
    return attended_output.astype(jnp.bfloat16).reshape(TOKENS, DH)

def reference(queries, keys, values, w_out, head_kind, band_offsets):

    def one_head(head_items):
        query_rows, key_rows, value_rows, head_type = head_items
        temporal = head_type == 1
        offsets = jnp.where(temporal, band_offsets[1], band_offsets[0])
        query_rows = jnp.where(temporal, to_temporal(query_rows), query_rows)
        key_rows = jnp.where(temporal, to_temporal(key_rows), key_rows)
        value_rows = jnp.where(temporal, to_temporal(value_rows), value_rows)
        attended_output = band_attend(query_rows, key_rows, value_rows, offsets)
        return jnp.where(temporal, from_temporal(attended_output), attended_output)
    query_heads = queries.reshape(TOKENS, HEADS, DH).transpose(1, 0, 2)
    key_heads = keys.reshape(TOKENS, HEADS, DH).transpose(1, 0, 2)
    value_heads = values.reshape(TOKENS, HEADS, DH).transpose(1, 0, 2)
    per_head = lax.map(one_head, (query_heads, key_heads, value_heads, head_kind))
    attended_output = per_head.transpose(1, 0, 2).reshape(TOKENS, HEADS * DH)
    group_width = HEAD_DEV * DH

    def add_group(total, group):
        group_data = lax.dynamic_slice_in_dim(attended_output, group * group_width, group_width, 1)
        group_rows = lax.dynamic_slice_in_dim(w_out, group * group_width, group_width, 0)
        partial_value = jnp.dot(group_data, group_rows, preferred_element_type=jnp.float32).astype(jnp.bfloat16)
        partial_value = lax.optimization_barrier(partial_value)
        return (total + partial_value.astype(jnp.float32), None)
    total, unused = lax.scan(add_group, jnp.zeros((TOKENS, D), jnp.float32), jnp.arange(N_HEAD, dtype=jnp.int32))
    return total.astype(jnp.bfloat16)
```

```python
import functools
import math

import jax
import jax.numpy as jnp
from jax import lax
from jax.experimental import pallas as pl
from jax.experimental.pallas import tpu as pltpu
from jax.sharding import PartitionSpec as P

DH = 128
FRAMES = 16
BLK = 256
CHUNK = 16
LIMIT = 48 * 1024 * 1024


class Plan:
    def __init__(self, seq_count, tok, head_dev, koff):
        self.n = seq_count
        self.pairs = seq_count // 2
        self.tok = tok
        self.hd = head_dev
        self.cap = head_dev - 1
        self.s = (head_dev + 1) // 2
        self.koff = koff
        positions = tok * seq_count // FRAMES
        self.span_rows = min(tok, positions)
        self.spans = tok // self.span_rows
        self.quota = self.span_rows // seq_count
        self.halves = positions // self.span_rows
        self.piece = self.spans * 2 * self.quota
        self.groups = 2 * self.quota // CHUNK
        self.unit = self.pairs * self.spans * CHUNK
        self.blocks = tok // BLK
        self.total = self.blocks * seq_count
        self.at_pair = 0
        self.at_side = 1
        self.at_order = 2
        self.at_kind = self.at_order + 2 * self.s
        self.at_band = self.at_kind + 2 * self.s


def table_of(plan, head_kind, band_offsets):
    rank = lax.axis_index("seq")
    kinds = lax.dynamic_slice_in_dim(head_kind, lax.axis_index("head") * plan.hd, plan.hd)
    places = jnp.arange(plan.hd, dtype=jnp.int32)
    spatial = jnp.min(jnp.where(kinds == 0, places, plan.hd - 1))
    low = jnp.arange(plan.cap, dtype=jnp.int32)
    order = low + (low >= spatial).astype(jnp.int32)
    kind = jnp.where(low < spatial, kinds[:-1], kinds[1:])
    rest = 2 * plan.s - plan.cap
    return jnp.concatenate(
        [
            (rank // 2).reshape(1).astype(jnp.int32),
            (rank % 2).reshape(1).astype(jnp.int32),
            order,
            jnp.broadcast_to(spatial, (rest,)),
            kind.astype(jnp.int32),
            jnp.zeros((rest,), jnp.int32),
            band_offsets.reshape(-1),
        ]
    )


def pair_permute(plan, cells, k):
    return lax.ppermute(
        cells,
        "seq",
        [(2 * p + y, 2 * (p ^ k) + y) for p in range(plan.pairs) for y in range(2)],
    )


def side_permute(plan, cells):
    return lax.ppermute(cells, "seq", [(i, i ^ 1) for i in range(plan.n)])


def call(body, plan, grid, in_specs, out_specs, out_shape, name, scratch=(), cost=None):
    return pl.pallas_call(
        body,
        grid_spec=pltpu.PrefetchScalarGridSpec(
            num_scalar_prefetch=1,
            grid=grid,
            in_specs=in_specs,
            out_specs=out_specs,
            scratch_shapes=list(scratch),
        ),
        out_shape=out_shape,
        compiler_params=pltpu.CompilerParams(
            vmem_limit_bytes=LIMIT, dimension_semantics=("arbitrary",) * len(grid)
        ),
        cost_estimate=cost,
        name=name,
    )


def copy_cost(count):
    return pl.CostEstimate(flops=0, bytes_accessed=count, transcendentals=0)


def shape(*dims):
    return jax.ShapeDtypeStruct(dims, jnp.bfloat16)


def split_pieces(plan, table, cells, name):
    r2 = 2 * plan.quota

    def body(info, x_ref, *outs):
        pair = info[plan.at_pair]
        for k, out in enumerate(outs):
            for sp in range(plan.spans):
                start = pl.multiple_of(sp * plan.span_rows + (pair ^ k) * r2, r2)
                out[0, sp * r2 : (sp + 1) * r2, :] = x_ref[pl.ds(start, r2), :]

    return call(
        body,
        plan,
        (plan.cap,),
        [pl.BlockSpec((plan.tok, DH), lambda j, info: (0, info[plan.at_order + j]))],
        [pl.BlockSpec((1, plan.piece, DH), lambda j, info: (j, 0, 0))] * plan.pairs,
        [shape(plan.cap, plan.piece, DH)] * plan.pairs,
        name,
        cost=copy_cost(2 * 2 * plan.cap * plan.tok * DH),
    )(table, cells)


def share_slots(plan, table, pieces, cells, name):
    r2 = 2 * plan.quota
    s = plan.s

    def slot_of(t, info):
        side = info[plan.at_side]
        return jnp.where(t < s, (1 - side) * s + t, side * s + t - s)

    def body(info, *refs):
        pieces_in, x_ref = refs[: plan.pairs], refs[plan.pairs]
        send, keep = refs[plan.pairs + 1 :]
        t = pl.program_id(0)
        kind = info[plan.at_kind + slot_of(t, info)]

        def write(out):
            @pl.when(kind == 1)
            def _():
                for k in range(plan.pairs):
                    for sp in range(plan.spans):
                        for c in range(plan.groups):
                            row = c * plan.unit + (k * plan.spans + sp) * CHUNK
                            out[0, row : row + CHUNK, :] = pieces_in[k][
                                0, sp * r2 + c * CHUNK : sp * r2 + (c + 1) * CHUNK, :
                            ]

            @pl.when(kind != 1)
            def _():
                out[0] = x_ref[...]

        @pl.when(t < s)
        def _():
            write(send)

        @pl.when(t >= s)
        def _():
            write(keep)

    return call(
        body,
        plan,
        (2 * s,),
        [
            pl.BlockSpec(
                (1, plan.piece, DH),
                lambda t, info: (jnp.minimum(slot_of(t, info), plan.cap - 1), 0, 0),
            )
        ]
        * plan.pairs
        + [
            pl.BlockSpec(
                (plan.tok, DH), lambda t, info: (0, info[plan.at_order + slot_of(t, info)])
            )
        ],
        [
            pl.BlockSpec((1, plan.tok, DH), lambda t, info: (jnp.minimum(t, s - 1), 0, 0)),
            pl.BlockSpec((1, plan.tok, DH), lambda t, info: (jnp.maximum(t - s, 0), 0, 0)),
        ],
        [shape(s, plan.tok, DH)] * 2,
        name,
        cost=copy_cost(2 * 3 * 2 * s * plan.tok * DH),
    )(table, *pieces, cells)


def block_sources(plan, kind, side):
    sources = []
    for b in range(2 * plan.blocks):
        if kind == 1 and plan.halves == 1:
            first = b * plan.unit
            sources.append([(0, first, plan.unit), (1, first, plan.unit)])
        elif kind == 1:
            per = plan.quota // CHUNK
            d, rest = divmod(b, plan.halves * per)
            h, c = divmod(rest, per)
            sources.append([(0 if h == side else 1, (d * per + c) * BLK, BLK)])
        else:
            part, row = divmod(b, plan.blocks)
            sources.append([(0 if part == side else 1, row * BLK, BLK)])
    return sources


def each_case(plan, info, slot, use):
    kind = info[plan.at_kind + slot]
    side = info[plan.at_side]
    for a_kind in range(2):
        for a_side in range(2):

            @pl.when((kind == a_kind) & (side == a_side))
            def _():
                use(block_sources(plan, a_kind, a_side))


def join_blocks(plan, table, own, other, name):
    s = plan.s

    def body(info, own_ref, other_ref, low, high):
        slot = info[plan.at_side] * s + pl.program_id(0)

        def use(sources):
            for b, parts in enumerate(sources):
                out = low if b < plan.blocks else high
                row = (b % plan.blocks) * BLK
                for part, first, rows in parts:
                    src = own_ref if part == 0 else other_ref
                    out[0, row : row + rows, :] = src[0, first : first + rows, :]
                    row += rows

        each_case(plan, info, slot, use)

    spec = pl.BlockSpec((1, plan.tok, DH), lambda t, info: (t, 0, 0))
    return call(
        body,
        plan,
        (s,),
        [spec] * 2,
        [spec] * 2,
        [shape(s, plan.tok, DH)] * 2,
        name,
        cost=copy_cost(2 * 4 * s * plan.tok * DH),
    )(table, own, other)


def attend(plan, table, q_parts, k_parts, v_parts):
    s, koff, tok = plan.s, plan.koff, plan.tok
    factor = math.log2(math.e) / math.sqrt(DH)

    def body(info, q_own, q_oth, k0, k1, k2, k3, v0, v1, v2, v3, o_own, o_oth, qs, ks, vs, os):
        t = pl.program_id(0)
        side = info[plan.at_side]
        slot = side * s + t
        kind = info[plan.at_kind + slot]
        first_block = info[plan.at_pair] * (2 * plan.blocks)

        @pl.when(t == 0)
        def _():
            vs[:, DH:] = jnp.ones((4 * tok, DH), jnp.bfloat16)

        for i, (k_ref, v_ref) in enumerate(((k0, v0), (k1, v1), (k2, v2), (k3, v3))):
            ks[i * tok : (i + 1) * tok, :] = k_ref[0]
            vs[i * tok : (i + 1) * tok, :DH] = v_ref[0]

        def load(sources):
            for b, parts in enumerate(sources):
                row = b * BLK
                for part, first, rows in parts:
                    src = q_own if part == 0 else q_oth
                    qs[row : row + rows, :] = src[0, first : first + rows, :]
                    row += rows

        each_case(plan, info, slot, load)

        def block(b):
            q = qs[pl.ds(pl.multiple_of(b * BLK, BLK), BLK), :]
            rows, drops = [], []
            for j in range(koff):
                goal = b + info[plan.at_band + kind * koff + j]
                ok = (first_block + goal >= 0) & (first_block + goal < plan.total)
                rows.append(pl.multiple_of((jnp.where(ok, goal, b) + plan.blocks) * BLK, BLK))
                drops.append(jnp.where(ok, 0.0, 1e30).astype(jnp.float32))
            keys = jnp.concatenate([ks[pl.ds(r, BLK), :] for r in rows], axis=0)
            scores = lax.dot_general(
                q, keys, (((1,), (1,)), ((), ())), preferred_element_type=jnp.float32
            )
            top = jnp.max(scores, axis=1, keepdims=True) * factor
            probs = jnp.concatenate(
                [
                    jnp.exp2(scores[:, j * BLK : (j + 1) * BLK] * factor - (top + drops[j])).astype(
                        jnp.bfloat16
                    )
                    for j in range(koff)
                ],
                axis=1,
            )
            vals = jnp.concatenate([vs[pl.ds(r, BLK), :] for r in rows], axis=0)
            mix = jnp.dot(probs, vals, preferred_element_type=jnp.float32)
            os[pl.ds(pl.multiple_of(b * BLK, BLK), BLK), :] = (mix[:, :DH] / mix[:, DH:]).astype(
                jnp.bfloat16
            )

        @pl.loop(0, plan.blocks)
        def _(i):
            block(2 * i)
            block(2 * i + 1)

        def store(sources):
            for b, parts in enumerate(sources):
                row = b * BLK
                for part, first, rows in parts:
                    dst = o_own if part == 0 else o_oth
                    dst[0, first : first + rows, :] = os[row : row + rows, :]
                    row += rows

        each_case(plan, info, slot, store)

    spec = pl.BlockSpec((1, tok, DH), lambda t, info: (t, 0, 0))
    pairs_count = s * 2 * plan.blocks * BLK * koff * BLK
    return call(
        body,
        plan,
        (s,),
        [spec] * 10,
        [spec] * 2,
        [shape(s, tok, DH)] * 2,
        "attend",
        scratch=[
            pltpu.VMEM((2 * tok, DH), jnp.bfloat16),
            pltpu.VMEM((4 * tok, DH), jnp.bfloat16),
            pltpu.VMEM((4 * tok, 2 * DH), jnp.bfloat16),
            pltpu.VMEM((2 * tok, DH), jnp.bfloat16),
        ],
        cost=pl.CostEstimate(
            flops=4 * pairs_count * DH,
            bytes_accessed=12 * 2 * s * tok * DH,
            transcendentals=pairs_count,
        ),
    )(table, *q_parts, *k_parts, *v_parts)


def return_pieces(plan, table, own, other):
    r2 = 2 * plan.quota
    s = plan.s

    def body(info, own_ref, oth_ref, *outs):
        j = pl.program_id(0)
        mine = j // s == info[plan.at_side]

        def write(src):
            for k, out in enumerate(outs):
                for sp in range(plan.spans):
                    for c in range(plan.groups):
                        row = c * plan.unit + (k * plan.spans + sp) * CHUNK
                        out[0, sp * r2 + c * CHUNK : sp * r2 + (c + 1) * CHUNK, :] = src[
                            0, row : row + CHUNK, :
                        ]

        @pl.when(mine)
        def _():
            write(own_ref)

        @pl.when(jnp.logical_not(mine))
        def _():
            write(oth_ref)

    spec = pl.BlockSpec((1, plan.tok, DH), lambda j, info: (j % s, 0, 0))
    return call(
        body,
        plan,
        (plan.cap,),
        [spec] * 2,
        [pl.BlockSpec((1, plan.piece, DH), lambda j, info: (j, 0, 0))] * plan.pairs,
        [shape(plan.cap, plan.piece, DH)] * plan.pairs,
        "return_pieces",
        cost=copy_cost(2 * 3 * plan.cap * plan.tok * DH),
    )(table, own, other)


def final_rows(plan, table, pieces, own, other):
    r2 = 2 * plan.quota
    s = plan.s

    def body(info, own_ref, oth_ref, *refs):
        pieces_in, out = refs[: plan.pairs], refs[plan.pairs]
        j = pl.program_id(0)
        pair = info[plan.at_pair]
        kind = info[plan.at_kind + j]
        mine = j // s == info[plan.at_side]

        @pl.when(kind == 1)
        def _():
            for k in range(plan.pairs):
                for sp in range(plan.spans):
                    start = pl.multiple_of(sp * plan.span_rows + (pair ^ k) * r2, r2)
                    out[pl.ds(start, r2), :] = pieces_in[k][0, sp * r2 : (sp + 1) * r2, :]

        @pl.when((kind != 1) & mine)
        def _():
            out[...] = own_ref[0]

        @pl.when((kind != 1) & jnp.logical_not(mine))
        def _():
            out[...] = oth_ref[0]

    spec = pl.BlockSpec((1, plan.tok, DH), lambda j, info: (j % s, 0, 0))
    piece = pl.BlockSpec(
        (1, plan.piece, DH), lambda j, info: (jnp.minimum(j, plan.cap - 1), 0, 0)
    )
    return call(
        body,
        plan,
        (plan.hd,),
        [spec] * 2 + [piece] * plan.pairs,
        pl.BlockSpec((plan.tok, DH), lambda j, info: (0, info[plan.at_order + j])),
        shape(plan.tok, plan.hd * DH),
        "final_rows",
        cost=copy_cost(2 * 4 * plan.hd * plan.tok * DH),
    )(table, own, other, *pieces)


def project(rows, weights):
    groups, r, c = rows.shape
    seq, _, _, d = weights.shape
    step = math.lcm(d, 256) // d

    def body(x_ref, w_ref, out):
        total = jnp.zeros((r, step * d), jnp.float32)
        for g in range(groups):
            w = jnp.concatenate([w_ref[i, g] for i in range(step)], axis=1)
            total += jnp.dot(x_ref[g], w, preferred_element_type=jnp.float32)
        out[...] = total.astype(jnp.bfloat16)

    return pl.pallas_call(
        body,
        grid=(seq // step,),
        in_specs=[
            pl.BlockSpec((groups, r, c), lambda i: (0, 0, 0)),
            pl.BlockSpec((step, groups, c, d), lambda i: (i, 0, 0, 0)),
        ],
        out_specs=pl.BlockSpec((r, step * d), lambda i: (0, i)),
        out_shape=shape(r, seq * d),
        compiler_params=pltpu.CompilerParams(vmem_limit_bytes=LIMIT),
        cost_estimate=pl.CostEstimate(
            flops=2 * groups * r * c * seq * d,
            bytes_accessed=2 * (groups * r * c + seq * groups * c * d + r * seq * d),
            transcendentals=0,
        ),
        name="project",
    )(rows, weights)


def body(queries, keys, values, w_out, head_kind, band_offsets):
    tok = queries.shape[0]
    plan = Plan(lax.axis_size("seq"), tok, queries.shape[1] // DH, band_offsets.shape[1])
    group_count = lax.axis_size("head")
    table = table_of(plan, head_kind, band_offsets)

    weights = lax.all_gather(w_out, ("seq", "head"), axis=0, tiled=False)
    weights = weights.reshape(plan.n, group_count, *w_out.shape)

    def exchange(cells, name):
        pieces = split_pieces(plan, table, cells, "split_" + name)
        moved = [pieces[0]] + [pair_permute(plan, pieces[k], k) for k in range(1, plan.pairs)]
        send, keep = share_slots(plan, table, moved, cells, "share_" + name)
        return keep, side_permute(plan, send)

    up = [(i, i + 2) for i in range(plan.n - 2)]
    down = [(i + 2, i) for i in range(plan.n - 2)]

    def extend(parts, name):
        low, high = join_blocks(plan, table, *parts, "join_" + name)
        return lax.ppermute(high, "seq", up), low, high, lax.ppermute(low, "seq", down)

    k_parts = extend(exchange(keys, "k"), "k")
    v_parts = extend(exchange(values, "v"), "v")
    q_parts = exchange(queries, "q")
    o_own, o_oth = attend(plan, table, q_parts, k_parts, v_parts)
    o_back = side_permute(plan, o_oth)
    pieces = return_pieces(plan, table, o_own, o_back)
    moved = [pieces[0]] + [pair_permute(plan, pieces[k], k) for k in range(1, plan.pairs)]
    rows = final_rows(plan, table, moved, o_own, o_back)
    token_rows = lax.all_to_all(
        rows.reshape(group_count, tok // group_count, plan.hd * DH),
        "head",
        split_axis=0,
        concat_axis=0,
        tiled=True,
    )
    return project(token_rows, weights)


def solution(mesh):
    return jax.shard_map(
        body,
        mesh=mesh,
        in_specs=(P("seq", "head"), P("seq", "head"), P("seq", "head"), P("head", "seq"), P(), P()),
        out_specs=P(("seq", "head"), None),
        check_vma=False,
    )
```

```python
import functools
import math

import jax
import jax.numpy as jnp
from jax import lax
from jax.experimental import pallas as pl
from jax.experimental.pallas import tpu as pltpu
from jax.sharding import PartitionSpec as P

DH = 128
FRAMES = 16
BLK = 256
CHUNK = 16
LIMIT = 48 * 1024 * 1024


class Plan:
    def __init__(self, seq_count, group_count, tok, head_dev, koff):
        self.n = seq_count
        self.g = group_count
        self.pairs = seq_count // 2
        self.tok = tok
        self.hd = head_dev
        self.cap = head_dev - 1
        self.s = (head_dev + 1) // 2
        self.koff = koff
        positions = tok * seq_count // FRAMES
        self.span_rows = min(tok, positions)
        self.spans = tok // self.span_rows
        self.quota = self.span_rows // seq_count
        self.halves = positions // self.span_rows
        self.piece = self.spans * 2 * self.quota
        self.groups = 2 * self.quota // CHUNK
        self.unit = self.pairs * self.spans * CHUNK
        self.blocks = tok // BLK
        self.total = self.blocks * seq_count
        self.pair_groups = [[2 * p + y for p in range(self.pairs)] for y in range(2)]

    def exchanged(self, wave):
        return len([j for j in (wave, self.s + wave) if j < self.cap])


class Info:
    def __init__(self, plan, place, kinds, bands):
        self.plan, self.kinds, self.bands = plan, kinds, bands
        self.pair, self.side, self.group = place[0], place[1], place[2]

    def spatial(self, group):
        found = self.plan.hd - 1
        for j in reversed(range(self.plan.hd)):
            found = jnp.where(self.kinds[group * self.plan.hd + j] == 0, j, found)
        return found

    def head(self, slot, group=None):
        spatial = self.spatial(self.group if group is None else group)
        return jnp.where(
            slot < self.plan.cap, slot + jnp.where(slot >= spatial, 1, 0), spatial
        )

    def kind(self, slot):
        kind = self.kinds[self.group * self.plan.hd + self.head(slot)]
        return jnp.where(slot < self.plan.cap, kind, 0)


SCALARS = 3


def call(body, plan, scalars, grid, in_specs, out_specs, out_shape, name, scratch=(), cost=None):
    def with_info(*refs):
        body(Info(plan, *refs[:SCALARS]), *refs[SCALARS:])

    def wrap(spec):
        index_map = spec.index_map
        arity = len(grid)
        return pl.BlockSpec(
            spec.block_shape,
            lambda *args: index_map(*args[:arity], Info(plan, *args[arity:])),
        )

    in_specs = [wrap(x) for x in in_specs]
    out_specs = [wrap(x) for x in out_specs] if isinstance(out_specs, list) else wrap(out_specs)
    run = pl.pallas_call(
        with_info,
        grid_spec=pltpu.PrefetchScalarGridSpec(
            num_scalar_prefetch=SCALARS,
            grid=grid,
            in_specs=in_specs,
            out_specs=out_specs,
            scratch_shapes=list(scratch),
        ),
        out_shape=out_shape,
        compiler_params=pltpu.CompilerParams(
            vmem_limit_bytes=LIMIT, dimension_semantics=("arbitrary",) * len(grid)
        ),
        cost_estimate=cost,
        name=name,
    )
    return functools.partial(run, *scalars)


def copy_cost(count):
    return pl.CostEstimate(flops=0, bytes_accessed=count, transcendentals=0)


def shape(*dims):
    return jax.ShapeDtypeStruct(dims, jnp.bfloat16)


def whole(*dims):
    return pl.BlockSpec(dims, lambda *_: (0,) * len(dims))


def side_permute(plan, cells):
    return lax.ppermute(cells, "seq", [(i, i ^ 1) for i in range(plan.n)])


def pair_permute(plan, cells, k):
    return lax.ppermute(
        cells,
        "seq",
        [(2 * p + y, 2 * (p ^ k) + y) for p in range(plan.pairs) for y in range(2)],
    )


def pair_exchange(plan, pieces):
    return [pieces[0]] + [pair_permute(plan, pieces[k], k) for k in range(1, plan.pairs)]


def slot_spec(plan, slot_of):
    return pl.BlockSpec((plan.tok, DH), lambda t, info: (0, info.head(slot_of(t, info))))


def split_pieces(plan, scalars, cells, name):
    r2 = 2 * plan.quota

    def body(info, x_ref, *outs):
        for k, out in enumerate(outs):
            for sp in range(plan.spans):
                start = pl.multiple_of(sp * plan.span_rows + (info.pair ^ k) * r2, r2)
                out[0, sp * r2 : (sp + 1) * r2, :] = x_ref[pl.ds(start, r2), :]

    return call(
        body,
        plan,
        scalars,
        (plan.cap,),
        [slot_spec(plan, lambda t, info: t)],
        [pl.BlockSpec((1, plan.piece, DH), lambda j, info: (j, 0, 0))] * plan.pairs,
        [shape(plan.cap, plan.piece, DH)] * plan.pairs,
        "split_" + name,
        cost=copy_cost(4 * plan.cap * plan.tok * DH),
    )(cells)


def share_slots(plan, scalars, pieces, cells, name):
    r2 = 2 * plan.quota
    s = plan.s

    def slot_of(t, info):
        return jnp.where(t < s, (1 - info.side) * s + t, info.side * s + t - s)

    def body(info, *refs):
        pieces_in, x_ref = refs[: plan.pairs], refs[plan.pairs]
        send, keep = refs[plan.pairs + 1 :]
        t = pl.program_id(0)
        kind = info.kind(slot_of(t, info))

        def write(out):
            @pl.when(kind == 1)
            def _():
                for k in range(plan.pairs):
                    for sp in range(plan.spans):
                        for c in range(plan.groups):
                            row = c * plan.unit + (k * plan.spans + sp) * CHUNK
                            first = sp * r2 + c * CHUNK
                            out[0, row : row + CHUNK, :] = pieces_in[k][0, first : first + CHUNK, :]

            @pl.when(kind != 1)
            def _():
                out[0] = x_ref[...]

        @pl.when(t < s)
        def _():
            write(send)

        @pl.when(t >= s)
        def _():
            write(keep)

    piece = pl.BlockSpec(
        (1, plan.piece, DH), lambda t, info: (jnp.minimum(slot_of(t, info), plan.cap - 1), 0, 0)
    )
    return call(
        body,
        plan,
        scalars,
        (2 * s,),
        [piece] * plan.pairs + [slot_spec(plan, slot_of)],
        [
            pl.BlockSpec((1, plan.tok, DH), lambda t, info: (jnp.minimum(t, s - 1), 0, 0)),
            pl.BlockSpec((1, plan.tok, DH), lambda t, info: (jnp.maximum(t - s, 0), 0, 0)),
        ],
        [shape(s, plan.tok, DH)] * 2,
        "share_" + name,
        cost=copy_cost(12 * s * plan.tok * DH),
    )(*pieces, cells)


def block_sources(plan, kind, side):
    sources = []
    for b in range(2 * plan.blocks):
        if kind == 1 and plan.halves == 1:
            first = b * plan.unit
            sources.append([(0, first, plan.unit), (1, first, plan.unit)])
        elif kind == 1:
            per = plan.quota // CHUNK
            d, rest = divmod(b, plan.halves * per)
            h, c = divmod(rest, per)
            sources.append([(0 if h == side else 1, (d * per + c) * BLK, BLK)])
        else:
            part, row = divmod(b, plan.blocks)
            sources.append([(0 if part == side else 1, row * BLK, BLK)])
    return sources


def each_case(plan, info, kind, use):
    for a_kind in range(2):
        for a_side in range(2):

            @pl.when((kind == a_kind) & (info.side == a_side))
            def _():
                use(block_sources(plan, a_kind, a_side))


def join_blocks(plan, scalars, own, other, name):
    s = plan.s

    def body(info, own_ref, other_ref, low, high):
        def use(sources):
            for b, parts in enumerate(sources):
                out = low if b < plan.blocks else high
                row = (b % plan.blocks) * BLK
                for part, first, rows in parts:
                    src = own_ref if part == 0 else other_ref
                    out[0, row : row + rows, :] = src[0, first : first + rows, :]
                    row += rows

        each_case(plan, info, info.kind(info.side * s + pl.program_id(0)), use)

    spec = pl.BlockSpec((1, plan.tok, DH), lambda t, info: (t, 0, 0))
    return call(
        body,
        plan,
        scalars,
        (s,),
        [spec] * 2,
        [spec] * 2,
        [shape(s, plan.tok, DH)] * 2,
        "join_" + name,
        cost=copy_cost(8 * s * plan.tok * DH),
    )(own, other)


def attend(plan, scalars, wave, q_parts, k_parts, v_parts):
    koff, tok = plan.koff, plan.tok
    factor = math.log2(math.e) / math.sqrt(DH)

    def body(info, q_own, q_oth, k0, k1, k2, k3, v0, v1, v2, v3, o_own, o_oth, qs, ks, vs, os):
        kind = info.kind(info.side * plan.s + wave)
        first_block = info.pair * (2 * plan.blocks)
        vs[:, DH:] = jnp.ones((4 * tok, DH), jnp.bfloat16)
        for i, (k_ref, v_ref) in enumerate(((k0, v0), (k1, v1), (k2, v2), (k3, v3))):
            ks[i * tok : (i + 1) * tok, :] = k_ref[0]
            vs[i * tok : (i + 1) * tok, :DH] = v_ref[0]

        def load(sources):
            for b, pieces in enumerate(sources):
                row = b * BLK
                for part, first, rows in pieces:
                    src = q_own if part == 0 else q_oth
                    qs[row : row + rows, :] = src[0, first : first + rows, :]
                    row += rows

        each_case(plan, info, kind, load)

        def block(b):
            q = qs[pl.ds(pl.multiple_of(b * BLK, BLK), BLK), :]
            rows, drops = [], []
            for j in range(koff):
                goal = b + info.bands[kind * koff + j]
                ok = (first_block + goal >= 0) & (first_block + goal < plan.total)
                rows.append(pl.multiple_of((jnp.where(ok, goal, b) + plan.blocks) * BLK, BLK))
                drops.append(jnp.where(ok, 0.0, 1e30).astype(jnp.float32))
            keys = jnp.concatenate([ks[pl.ds(r, BLK), :] for r in rows], axis=0)
            scores = lax.dot_general(
                q, keys, (((1,), (1,)), ((), ())), preferred_element_type=jnp.float32
            )
            top = jnp.max(scores, axis=1, keepdims=True) * factor
            probs = jnp.concatenate(
                [
                    jnp.exp2(scores[:, j * BLK : (j + 1) * BLK] * factor - (top + drops[j])).astype(
                        jnp.bfloat16
                    )
                    for j in range(koff)
                ],
                axis=1,
            )
            vals = jnp.concatenate([vs[pl.ds(r, BLK), :] for r in rows], axis=0)
            mix = jnp.dot(probs, vals, preferred_element_type=jnp.float32)
            os[pl.ds(pl.multiple_of(b * BLK, BLK), BLK), :] = (mix[:, :DH] / mix[:, DH:]).astype(
                jnp.bfloat16
            )

        @pl.loop(0, plan.blocks)
        def _(i):
            block(2 * i)
            block(2 * i + 1)

        def store(sources):
            for b, pieces in enumerate(sources):
                row = b * BLK
                for part, first, rows in pieces:
                    dst = o_own if part == 0 else o_oth
                    dst[first : first + rows, :] = os[row : row + rows, :]
                    row += rows

        each_case(plan, info, kind, store)

    spec = pl.BlockSpec((1, tok, DH), lambda *_: (wave, 0, 0))
    pairs_count = 2 * plan.blocks * BLK * koff * BLK
    return call(
        body,
        plan,
        scalars,
        (1,),
        [spec] * 10,
        [whole(tok, DH)] * 2,
        [shape(tok, DH)] * 2,
        f"attend_{wave}",
        scratch=[
            pltpu.VMEM((2 * tok, DH), jnp.bfloat16),
            pltpu.VMEM((4 * tok, DH), jnp.bfloat16),
            pltpu.VMEM((4 * tok, 2 * DH), jnp.bfloat16),
            pltpu.VMEM((2 * tok, DH), jnp.bfloat16),
        ],
        cost=pl.CostEstimate(
            flops=4 * pairs_count * DH,
            bytes_accessed=24 * tok * DH,
            transcendentals=pairs_count,
        ),
    )(*q_parts, *k_parts, *v_parts)


def return_wave(plan, scalars, wave, own, other):
    r2 = 2 * plan.quota
    count = plan.exchanged(wave)

    def body(info, own_ref, oth_ref, *outs):
        def write(i, src):
            for p, out in enumerate(outs):
                for sp in range(plan.spans):
                    for c in range(plan.groups):
                        row = c * plan.unit + (p * plan.spans + sp) * CHUNK
                        first = sp * r2 + c * CHUNK
                        out[i, first : first + CHUNK, :] = src[row : row + CHUNK, :]

        for side in range(2):

            @pl.when(info.side == side)
            def _():
                for i in range(count):
                    write(i, own_ref if i == side else oth_ref)

    return call(
        body,
        plan,
        scalars,
        (1,),
        [whole(plan.tok, DH)] * 2,
        [whole(count, plan.piece, DH)] * plan.pairs,
        [shape(count, plan.piece, DH)] * plan.pairs,
        f"return_{wave}",
        cost=copy_cost(8 * plan.tok * DH),
    )(own, other)


def final_wave(plan, scalars, wave, pieces, own, other):
    r2 = 2 * plan.quota
    count = plan.exchanged(wave)

    def body(info, own_ref, oth_ref, *refs):
        pieces_in, out = refs[: plan.pairs], refs[plan.pairs]
        for i in range(2):
            lanes = slice(i * DH, (i + 1) * DH)
            kind = info.kind(wave + i * plan.s)

            if i < count:

                @pl.when(kind == 1)
                def _():
                    for p in range(plan.pairs):
                        for sp in range(plan.spans):
                            start = pl.multiple_of(sp * plan.span_rows + (info.pair ^ p) * r2, r2)
                            out[pl.ds(start, r2), lanes] = pieces_in[p][
                                i, sp * r2 : (sp + 1) * r2, :
                            ]

            @pl.when((kind != 1) & (info.side == i))
            def _():
                out[:, lanes] = own_ref[...]

            @pl.when((kind != 1) & (info.side != i))
            def _():
                out[:, lanes] = oth_ref[...]

    return call(
        body,
        plan,
        scalars,
        (1,),
        [whole(plan.tok, DH)] * 2 + [whole(count, plan.piece, DH)] * plan.pairs,
        whole(plan.tok, 2 * DH),
        shape(plan.tok, 2 * DH),
        f"final_{wave}",
        cost=copy_cost(12 * plan.tok * DH),
    )(own, other, *pieces)


def after(place, done):
    return lax.optimization_barrier((place, done))[0]


def hold(done, value):
    return lax.optimization_barrier((done, value))[1]


def project(plan, scalars, waves, weights):
    groups, r, _ = waves[0].shape
    _, _, _, c, d = weights[0].shape
    pairs, lots = plan.pairs, []
    for lot in weights:
        lots.append((sum(x[1] for x in lots), lot.shape[2]))

    def pair_of(m, info):
        far, shift, pair = pairs // 2, 0, info.pair
        while far:
            pair = pair ^ (((m >> shift) & 1) * far)
            far, shift = far // 2, shift + 1
        return pair

    def body(info, *refs):
        ins, ws, out, xs = refs[: len(waves)], refs[len(waves) : -2], refs[-2], refs[-1]

        @pl.when(pl.program_id(0) == 0)
        def _():
            for g in range(groups):
                for wave, x_ref in enumerate(ins):
                    for i in range(2):
                        slot = wave + i * plan.s
                        if slot < plan.hd:
                            head = info.head(slot, g)
                            xs[g * plan.hd + head] = x_ref[g, :, i * DH : (i + 1) * DH]

        def multiply(w_ref):
            total = jnp.zeros((r, 2 * d), jnp.float32)
            for g in range(groups):
                x = jnp.concatenate([xs[g * plan.hd + h] for h in range(plan.hd)], axis=1)
                w = jnp.concatenate([w_ref[y, g, 0] for y in range(2)], axis=1)
                total += jnp.dot(x, w, preferred_element_type=jnp.float32)
            out[...] = total.astype(jnp.bfloat16).reshape(out.shape)

        m = pl.program_id(0)
        for w_ref, (first, length) in zip(ws, lots):

            @pl.when((m >= first) & (m < first + length))
            def _():
                multiply(w_ref)

    aligned = 2 * d % DH == 0
    if aligned:
        out_spec = pl.BlockSpec((r, 2 * d), lambda m, info: (0, pair_of(m, info)))
        out_shape = shape(r, 2 * pairs * d)
    else:
        out_spec = pl.BlockSpec((1, r, 2 * d), lambda m, info: (pair_of(m, info), 0, 0))
        out_shape = shape(pairs, r, 2 * d)
    result = call(
        body,
        plan,
        scalars,
        (pairs,),
        [whole(groups, r, 2 * DH)] * len(waves)
        + [
            pl.BlockSpec(
                (2, groups, 1, c, d),
                lambda m, info, first=first, length=length: (
                    0,
                    0,
                    jnp.clip(m - first, 0, length - 1),
                    0,
                    0,
                ),
            )
            for first, length in lots
        ],
        out_spec,
        out_shape,
        "project",
        scratch=[pltpu.VMEM((groups * plan.hd, r, DH), jnp.bfloat16)],
        cost=pl.CostEstimate(
            flops=4 * groups * r * c * pairs * d,
            bytes_accessed=2 * (groups * r * c + 2 * pairs * groups * c * d + 2 * r * pairs * d),
            transcendentals=0,
        ),
    )(*waves, *weights)
    return result if aligned else result.transpose(1, 0, 2).reshape(r, 2 * pairs * d)


def body(queries, keys, values, w_out, head_kind, band_offsets):
    tok = queries.shape[0]
    plan = Plan(
        lax.axis_size("seq"),
        lax.axis_size("head"),
        tok,
        queries.shape[1] // DH,
        band_offsets.shape[1],
    )
    rank = lax.axis_index("seq")
    place = jnp.stack([rank >> 1, rank & 1, lax.axis_index("head")]).astype(jnp.int32)
    scalars = (place, head_kind, band_offsets.reshape(-1))
    up = [(i, i + 2) for i in range(plan.n - 2)]
    down = [(i + 2, i) for i in range(plan.n - 2)]

    order = place

    def step(run, *args):
        nonlocal order
        out = run(plan, (order, *scalars[1:]), *args)
        order = after(order, out)
        return out

    near = [
        [(2 * p + y) * plan.g + g for y in range(2) for g in range(plan.g)]
        for p in range(plan.pairs)
    ]

    def spread(lot):
        lot_all = lax.all_gather(lot, ("seq", "head"), axis=0, axis_index_groups=near)
        return lot_all.reshape(2, plan.g, *lot.shape)

    shards, far = w_out[None], plan.pairs // 2
    weights = [spread(shards)]
    coming = pair_permute(plan, shards, far)

    def more_shards():
        nonlocal shards, coming, far, order
        if far:
            arrived = hold(order, coming)
            weights.append(spread(arrived))
            far //= 2
            if far:
                shards = jnp.concatenate([shards, arrived], axis=0)
                order = after(order, shards)
                coming = pair_permute(plan, shards, far)
            else:
                order = after(order, arrived)

    def share(moved, cells, name):
        send, keep = step(share_slots, moved, cells, name)
        return keep, side_permute(plan, send)

    def extend(keep, other, name):
        low, high = step(join_blocks, keep, other, name)
        return lax.ppermute(high, "seq", up), low, high, lax.ppermute(low, "seq", down)

    moved_k = pair_exchange(plan, step(split_pieces, keys, "k"))
    moved_v = pair_exchange(plan, step(split_pieces, values, "v"))
    more_shards()
    k_parts = share(moved_k, keys, "k")
    moved_q = pair_exchange(plan, step(split_pieces, queries, "q"))
    while far:
        more_shards()
    v_parts = share(moved_v, values, "v")
    k_parts = extend(*k_parts, "k")
    q_parts = share(moved_q, queries, "q")
    v_parts = extend(*v_parts, "v")

    backs, returned, rows = [], [], []

    def attention(w):
        own, oth = step(attend, w, q_parts, k_parts, v_parts)
        backs.append((own, side_permute(plan, oth)))

    def give_back(w):
        returned.append(pair_exchange(plan, step(return_wave, w, *backs[w])))

    def finish(w):
        out = step(final_wave, w, returned[w], *backs[w])
        rows.append(
            lax.all_to_all(
                out.reshape(plan.g, tok // plan.g, 2 * DH),
                "head",
                split_axis=0,
                concat_axis=0,
                tiled=True,
            )
        )

    attention(0)
    for w in range(plan.s):
        if w + 1 < plan.s:
            attention(w + 1)
        give_back(w)
        if w:
            finish(w - 1)
    finish(plan.s - 1)
    return project(plan, scalars, rows, weights)


def solution(mesh):
    return jax.shard_map(
        body,
        mesh=mesh,
        in_specs=(P("seq", "head"), P("seq", "head"), P("seq", "head"), P("head", "seq"), P(), P()),
        out_specs=P(("seq", "head"), None),
        check_vma=False,
    )
```
